32 devices in a mesh: runs: 2 (over y), seg: 4 (over z), blk: 4 (over x, core).
Axes of the slice: x: 2, y: 2, z: 4, core: 2. Of those that a mesh axis runs over, the one named last changes fastest.
Arguments:
- bond_tensor: bfloat16 [8, 64, 64, 512], P(('runs', 'seg'), 'blk'), parts along dimension 0, may hold values from -36 to 36
- left_env: bfloat16 [8, 64, 64, 640], P(('runs', 'seg'), 'blk'), parts along dimension 0, may hold values from -0.75 to 0.75
- right_env: bfloat16 [8, 64, 64, 640], P(('runs', 'seg'), 'blk'), parts along dimension 0, may hold values from -0.25 to 0.25
- kept_dims: int32 [8, 2, 64], P(('runs', 'seg'), None, 'blk'), parts along dimension 0, may hold values from 16 to 64
- sector_links: int32 [8, 64, 10], P(('runs', 'seg'), 'blk'), parts along dimension 0, may hold values from -1 to 1
- mpo_pair: bfloat16 [80, 80], replicated, may hold values from -0.625 to 0.625
Outputs:
- handed_env: bfloat16 [8, 64, 64, 640], P(('runs', 'seg'), 'blk'), parts along dimension 0
The draws below stay inside these ranges and needn't reach their ends.
There are 2 independent parts, one for each index of `runs`. The reference program is written for one: setup_inputs(seed, part) draws one part's arguments, and reference() takes and returns one part's arrays. A program takes and returns all parts, laid end to end along the dimension named above; an argument that names none is the same for every part. Nothing has to cross between parts.
All inputs are finite; a program needn't handle non-finite values.
Results may differ from the reference program's by a relative error of at most 0.0067.
Values may be sent and summed in bfloat16 or wider, within the bound.
A program may use at most 192 MiB of HBM per device.

```python
import math
import jax
import jax.numpy as jnp
from jax import lax

BS = 64
P_SIZE = 8
W = 10
ITERS = 1
SECT = 64
BONDS = 4
COUNT = 2097152


def draw_bond_tensor(key, part):
    key = jax.random.fold_in(key, 11)
    base_key, row_key = jax.random.split(key)
    shape = (BONDS, SECT, BS, P_SIZE * BS)
    sector_pos = jnp.arange(SECT, dtype=jnp.float32).reshape(1, SECT, 1, 1) / (SECT - 1)
    row_factor = jnp.power(10.0, jax.random.uniform(row_key, (BONDS, SECT, BS, 1), jnp.float32, 0.0, 1.0))
    base = jnp.clip(jax.random.normal(base_key, shape, jnp.float32), -6.0, 6.0)
    ramp = 0.6 + 1.2 * sector_pos
    return (base * ramp * row_factor / 3.0).astype(jnp.bfloat16)


def touch_ends(array, key, smallest, largest):
    dims = array.shape
    index_at = [jax.random.randint(jax.random.fold_in(key, axis), (), 0, dims[axis]) for axis in range(len(dims))]
    array = array.at[tuple(index_at)].set(smallest)
    longest = dims.index(max(dims))
    index_at[longest] = (index_at[longest] + 1) % dims[longest]
    return array.at[tuple(index_at)].set(largest)


def level_of(stream_key, extent, pieces, least, largest):
    gain, own = 1.0, jax.random.fold_in(stream_key, 6)
    for axis_at, parts in pieces:
        steps = jnp.exp(jax.random.uniform(jax.random.fold_in(own, axis_at), (parts,), jnp.float32, least / len(pieces), largest / len(pieces)))
        gain = gain * jnp.repeat(steps, extent[axis_at] // parts).reshape([-1 if axis == axis_at else 1 for axis in range(len(extent))])
    return gain


def centred(key, dims, spread, limit, cuts=(), held_as=jnp.bfloat16):
    factor_of = level_of(key, dims, cuts, -0.22, 0.18) if cuts else 1.0
    array = jax.random.normal(key, dims, jnp.float32) * spread * factor_of
    return jnp.minimum(jnp.maximum(array, -limit), limit).astype(held_as)


def setup_inputs(seed: int = 0, part: int = 0) -> dict:
    keys = jax.random.split(jax.random.key(seed), 7)
    part_splits = jax.random.split(jax.random.fold_in(keys[6], part), 7)
    return {
        "bond_tensor": draw_bond_tensor(jax.random.fold_in(jax.random.fold_in(keys[6], part), 71), part),
        "left_env": centred(part_splits[1], (BONDS, SECT, BS, W * BS), BS ** -0.5, 0.75, ((0, 4), (1, 4))),
        "right_env": centred(part_splits[2], (BONDS, SECT, BS, W * BS), (W * BS) ** -0.5, 0.25, ((0, 4), (1, 4))),
        "kept_dims": touch_ends(jax.random.randint(part_splits[3], (BONDS, 2, SECT), BS // 4, BS + 1), jax.random.fold_in(part_splits[3], 1), BS // 4, BS).astype(jnp.int32),
        "sector_links": touch_ends(jax.random.randint(part_splits[4], (BONDS, SECT, W), -1, 2), jax.random.fold_in(part_splits[4], 1), -1, 1).astype(jnp.int32),
        "mpo_pair": centred(keys[5], (W * P_SIZE, W * P_SIZE), (W * P_SIZE) ** -0.5, 0.625),
    }


relax_step = 0.5
epsilon = 1e-06

def lift_state(left_block, current, links):
    padded = jnp.pad(current, ((1, 1), (0, 0), (0, 0), (0, 0)))
    source_idx = (jnp.arange(SECT, dtype=jnp.int32)[:, None] + 1 + links).astype(jnp.int32)
    picked = padded[source_idx].astype(jnp.float32)
    stacked = left_block.reshape(SECT, BS, W, BS).astype(jnp.float32)
    return jnp.einsum('jawc,jwcpb->jwapb', stacked, picked).astype(jnp.bfloat16)

def solve_bond(left_block, right_block, tensor_block, kept_block, links, mpo_pair):
    positions = jnp.arange(BS, dtype=jnp.int32)[None, :]
    row_keep = (positions < kept_block[0][:, None]).astype(jnp.float32)
    col_keep = (positions < kept_block[1][:, None]).astype(jnp.float32)
    keep_mask = row_keep[:, :, None, None] * col_keep[:, None, None, :]
    current = (tensor_block.reshape(SECT, BS, P_SIZE, BS).astype(jnp.float32) * keep_mask).astype(jnp.bfloat16)
    operator = mpo_pair.reshape(W, P_SIZE, W, P_SIZE).astype(jnp.float32)
    right_four = right_block.reshape(SECT, BS, W, BS).astype(jnp.float32)
    for sweep_step in range(ITERS):
        lifted = lift_state(left_block, current, links)
        channel_mix = jnp.einsum('jwapb,wpvr->jarvb', lifted.astype(jnp.float32), operator).astype(jnp.bfloat16)
        applied = jnp.einsum('jarvb,jcvb->jarc', channel_mix.astype(jnp.float32), right_four) * keep_mask
        trial_state = current.astype(jnp.float32) - relax_step * applied
        mean_square = jnp.sum(trial_state * trial_state) / COUNT
        current = (trial_state / jnp.sqrt(mean_square + epsilon)).astype(jnp.bfloat16)
    closing = lift_state(left_block, current, links)
    handed = jnp.einsum('japb,jwapc->jbwc', current.astype(jnp.float32), closing.astype(jnp.float32)) / math.sqrt(BS * P_SIZE)
    return handed.reshape(SECT, BS, W * BS).astype(jnp.bfloat16)

def reference(bond_tensor, left_env, right_env, kept_dims, sector_links, mpo_pair):
    right_next = jnp.roll(right_env, -1, axis=0)
    handed = lax.map(lambda bundle: solve_bond(bundle[0], bundle[1], bundle[2], bundle[3], bundle[4], mpo_pair), (left_env, right_next, bond_tensor, kept_dims, sector_links))
    return jnp.roll(handed, 1, axis=0)
```

```python
import math

import jax
import jax.numpy as jnp
from jax import lax
from jax.experimental import pallas as pl
from jax.experimental.pallas import tpu as pltpu
from jax.sharding import PartitionSpec as P

BS = 64
P_SIZE = 8
W = 10
LANES = P_SIZE * BS
WIDE = W * BS
MIX = W * 128

relax_step = 0.5
epsilon = 1e-06
lift_scale = 1024.0

f32 = jnp.float32
bf16 = jnp.bfloat16


def iota(shape, dim):
    return lax.broadcasted_iota(jnp.int32, shape, dim)


def dot(a, b, dims=((1,), (0,))):
    return lax.dot_general(a, b, (dims, ((), ())), preferred_element_type=f32)


def order_state(order_ref):
    row, lane = iota((LANES, LANES), 0), iota((LANES, LANES), 1)
    source = ((lane >> 4) & 7) * 64 + (lane >> 7) * 16 + (lane & 15)
    order_ref[...] = (row == source).astype(f32).astype(bf16)


def order_right(order_ref):
    row, lane = iota((WIDE, 128), 0), iota((WIDE, 128), 1)
    for b_hi in range(4):
        for v_hi in range(5):
            source = (v_hi * 2 + ((lane >> 4) & 1)) * 64 + b_hi * 16 + (lane & 15)
            at = (b_hi * 5 + v_hi) * 128
            order_ref[:, at : at + 128] = (row == source).astype(f32).astype(bf16)


def spread_operator(mpo_ref, mix_ref):
    size = W * P_SIZE
    rows = (iota((MIX, size), 1) == (iota((MIX, size), 0) >> 4)).astype(f32).astype(bf16)
    tall = dot(rows, mpo_ref[...]).astype(bf16)
    same = (iota((MIX, 128), 0) & 15) == (iota((MIX, 128), 1) & 15)
    row, lane = iota((size, 128), 0), iota((size, 128), 1)
    for r_hi in range(2):
        for v_hi in range(5):
            column = (v_hi * 2 + ((lane >> 4) & 1)) * 8 + r_hi * 4 + ((lane >> 5) & 3)
            pick = (row == column).astype(f32).astype(bf16)
            at = (r_hi * 5 + v_hi) * 128
            mix_ref[:, at : at + 128] = jnp.where(same, dot(tall, pick), 0.0).astype(bf16)


def keep_of(kept_ref, q, lanes):
    rows = iota((BS, lanes), 0) < kept_ref[0, q]
    columns = (iota((BS, lanes), 1) & 63) < kept_ref[1, q]
    return rows & columns


def lift_into(links_ref, q, left, state_ref, target_ref):
    for w in range(W):
        source = state_ref[q + 1 + links_ref[q, w]]
        out = dot(left[:, w * 64 : w * 64 + 64], source).astype(bf16)
        for k in range(4):
            target_ref[k * 64 : k * 64 + 64, w * 128 : w * 128 + 128] = out[:, k * 128 : k * 128 + 128]


def relax_sector(links_ref, kept_ref, q, left, right, bond, ordered_ref, order_ref, mix_ref, x_ref, rk_ref):
    lift_into(links_ref, q, left, ordered_ref, x_ref)
    mixed = dot(x_ref[...], mix_ref[...]).astype(bf16)
    spread = dot(right, order_ref[...]).astype(bf16)
    part = (iota((BS, 4 * WIDE), 1) >> 5) & 3
    for k in range(4):
        rk_ref[k * 64 : k * 64 + 64, :] = jnp.where(part == k, spread, jnp.zeros_like(spread))
    keep = keep_of(kept_ref, q, 256)
    halves = []
    for r_hi in range(2):
        rows = jnp.concatenate(
            [mixed[k * 64 : k * 64 + 64, r_hi * WIDE : r_hi * WIDE + WIDE] for k in range(4)], axis=1
        )
        applied = dot(rows, rk_ref[...], ((1,), (1,)))
        state = bond[:, r_hi * 256 : r_hi * 256 + 256].astype(f32)
        halves.append(jnp.where(keep, state - relax_step * applied, 0.0))
    return halves


def handed_sector(links_ref, q, left, state_ref, x_ref):
    lift_into(links_ref, q, left, state_ref, x_ref)
    own = state_ref[q + 1]
    stacked = jnp.concatenate([own[:, k * 128 : k * 128 + 128] for k in range(4)], axis=0)
    both = dot(stacked, x_ref[...], ((0,), (0,)))
    low = iota((BS, 128), 1) < 64
    out = []
    for w in range(0, W, 2):
        a0, b0 = both[:64, w * 128 : w * 128 + 128], both[64:, w * 128 : w * 128 + 128]
        a1, b1 = both[:64, w * 128 + 128 : w * 128 + 256], both[64:, w * 128 + 128 : w * 128 + 256]
        out.append(jnp.where(low, a0, b1) + pltpu.roll(jnp.where(low, a1, b0), 64, 1))
    return jnp.concatenate(out, axis=1)


def relax_kernel(links_ref, kept_ref, left_ref, right_ref, bond_ref, mpo_ref, state_ref, total_ref,
                 ordered_ref, lane_ref, order_ref, mix_ref, x_ref, rk_ref):
    step = pl.program_id(0)

    @pl.when(step == 0)
    def _():
        order_state(lane_ref)
        order_right(order_ref)
        spread_operator(mpo_ref, mix_ref)
        total_ref[...] = jnp.zeros_like(total_ref)

        def body(q, carry):
            keep = keep_of(kept_ref, q, LANES)
            held = jnp.where(keep, bond_ref[q].astype(f32), 0.0).astype(bf16)
            ordered_ref[q] = dot(held, lane_ref[...]).astype(bf16)
            return carry

        lax.fori_loop(0, bond_ref.shape[0], body, 0)

    halves = relax_sector(links_ref, ShiftedKept(kept_ref), step, left_ref[0], right_ref[0], bond_ref[step + 1],
                          ordered_ref, order_ref, mix_ref, x_ref, rk_ref)
    for r_hi, trial in enumerate(halves):
        total_ref[...] += trial * trial
        state_ref[0, :, r_hi * 256 : r_hi * 256 + 256] = (trial * lift_scale).astype(bf16)


class ShiftedKept:
    def __init__(self, ref):
        self.ref = ref

    def __getitem__(self, at):
        return self.ref[at[0], at[1] + 1]


def handed_kernel(links_ref, scale_ref, left_ref, state_ref, out_ref, x_ref):
    step = pl.program_id(0)
    value = handed_sector(links_ref, step, left_ref[0], state_ref, x_ref)
    out_ref[0] = (value * scale_ref[0, 0]).astype(bf16)


def padded(block, dim):
    count = lax.axis_size("blk")
    forward = [(i, i + 1) for i in range(count - 1)]
    backward = [(target, source) for source, target in forward]
    size = block.shape[dim]
    low = lax.ppermute(lax.slice_in_dim(block, size - 1, None, axis=dim), "blk", forward)
    high = lax.ppermute(lax.slice_in_dim(block, 0, 1, axis=dim), "blk", backward)
    return jnp.concatenate([low, block, high], axis=dim)


def shards(bond_tensor, left_env, right_env, kept_dims, sector_links, mpo_pair):
    count = lax.axis_size("seg")
    ring = [(i, (i + 1) % count) for i in range(count)]
    bond = padded(lax.ppermute(bond_tensor[0], "seg", ring), 0)
    left = lax.ppermute(left_env[0], "seg", ring)
    kept = padded(lax.ppermute(kept_dims[0], "seg", ring), 1)
    links = lax.ppermute(sector_links[0], "seg", ring)
    right = right_env[0]
    sectors = left.shape[0]
    smem = pl.BlockSpec(memory_space=pltpu.SMEM)
    per_sector = pl.BlockSpec((1, BS, WIDE), lambda q: (q, 0, 0))
    whole = pl.BlockSpec((sectors + 2, BS, LANES), lambda q: (0, 0, 0))
    params = pltpu.CompilerParams(vmem_limit_bytes=40 * 2**20)
    state, total = pl.pallas_call(
        relax_kernel,
        grid=(sectors,),
        out_shape=(jax.ShapeDtypeStruct((sectors, BS, LANES), bf16), jax.ShapeDtypeStruct((BS, 256), f32)),
        in_specs=[smem, smem, per_sector, per_sector, whole, pl.BlockSpec((80, 80), lambda q: (0, 0))],
        out_specs=(pl.BlockSpec((1, BS, LANES), lambda q: (q, 0, 0)), pl.BlockSpec((BS, 256), lambda q: (0, 0))),
        scratch_shapes=[
            pltpu.VMEM((sectors + 2, BS, LANES), bf16),
            pltpu.VMEM((LANES, LANES), bf16),
            pltpu.VMEM((WIDE, 4 * WIDE), bf16),
            pltpu.VMEM((MIX, MIX), bf16),
            pltpu.VMEM((256, MIX), bf16),
            pltpu.VMEM((256, 4 * WIDE), bf16),
        ],
        compiler_params=params,
    )(links, kept, left, right, bond, mpo_pair)
    total_count = sectors * lax.axis_size("blk") * BS * P_SIZE * BS
    mean_square = lax.psum(jnp.sum(total), "blk") / total_count
    scale = 1.0 / ((mean_square + epsilon) * (lift_scale * lift_scale * math.sqrt(BS * P_SIZE)))
    out = pl.pallas_call(
        handed_kernel,
        grid=(sectors,),
        out_shape=jax.ShapeDtypeStruct((sectors, BS, WIDE), bf16),
        in_specs=[smem, smem, per_sector, whole],
        out_specs=per_sector,
        scratch_shapes=[pltpu.VMEM((256, MIX), bf16)],
        compiler_params=params,
    )(links, scale.reshape(1, 1), left, padded(state, 0))
    return out[None]


def solution(mesh):
    return jax.shard_map(
        shards,
        mesh=mesh,
        in_specs=(
            P(("runs", "seg"), "blk", None, None),
            P(("runs", "seg"), "blk", None, None),
            P(("runs", "seg"), "blk", None, None),
            P(("runs", "seg"), None, "blk"),
            P(("runs", "seg"), "blk", None),
            P(),
        ),
        out_specs=P(("runs", "seg"), "blk", None, None),
        check_vma=False,
    )
```

```python
import functools
import math

import jax
import jax.numpy as jnp
from jax import lax
from jax.experimental import pallas as pl
from jax.experimental.pallas import tpu as pltpu
from jax.sharding import PartitionSpec as P

BS = 64
P_SIZE = 8
W = 10
LANES = P_SIZE * BS
WIDE = W * BS
MIX = W * 128

relax_step = 0.5
epsilon = 1e-06
lift_scale = 1024.0

f32 = jnp.float32
bf16 = jnp.bfloat16


def iota(shape, dim):
    return lax.broadcasted_iota(jnp.int32, shape, dim)


def dot(a, b, dims=((1,), (0,))):
    return lax.dot_general(a, b, (dims, ((), ())), preferred_element_type=f32)


def order_state(order_ref):
    row, lane = iota((LANES, LANES), 0), iota((LANES, LANES), 1)
    source = ((lane >> 4) & 7) * 64 + (lane >> 7) * 16 + (lane & 15)
    order_ref[...] = (row == source).astype(f32).astype(bf16)


def order_right(order_ref):
    row, lane = iota((WIDE, 128), 0), iota((WIDE, 128), 1)
    for b_hi in range(4):
        for v_hi in range(5):
            source = (v_hi * 2 + ((lane >> 4) & 1)) * 64 + b_hi * 16 + (lane & 15)
            at = (b_hi * 5 + v_hi) * 128
            order_ref[:, at : at + 128] = (row == source).astype(f32).astype(bf16)


def spread_operator(mpo_ref, mix_ref):
    size = W * P_SIZE
    rows = (iota((MIX, size), 1) == (iota((MIX, size), 0) >> 4)).astype(f32).astype(bf16)
    tall = dot(rows, mpo_ref[...]).astype(bf16)
    same = (iota((MIX, 128), 0) & 15) == (iota((MIX, 128), 1) & 15)
    row, lane = iota((size, 128), 0), iota((size, 128), 1)
    for r_hi in range(2):
        for v_hi in range(5):
            column = (v_hi * 2 + ((lane >> 4) & 1)) * 8 + r_hi * 4 + ((lane >> 5) & 3)
            pick = (row == column).astype(f32).astype(bf16)
            at = (r_hi * 5 + v_hi) * 128
            mix_ref[:, at : at + 128] = jnp.where(same, dot(tall, pick), 0.0).astype(bf16)


def keep_of(meta_ref, q, lanes):
    rows = iota((BS, lanes), 0) < meta_ref[q, W]
    columns = (iota((BS, lanes), 1) & 63) < meta_ref[q, W + 1]
    return rows & columns


def lift_into(meta_ref, q, left, state_ref, target_ref, base=0):
    for w in range(W):
        source = state_ref[q + 1 + meta_ref[q, w]]
        out = dot(left[:, w * 64 : w * 64 + 64], source).astype(bf16)
        for k in range(4):
            target_ref[base + k * 64 : base + k * 64 + 64, w * 128 : w * 128 + 128] = out[:, k * 128 : k * 128 + 128]


def relax_pair(meta_ref, g, left_ref, spread_ref, bond_ref, ordered_ref, mix_ref, x_ref, y_ref, rk_ref, state_ref, total_ref):
    for i in range(2):
        q = g * 2 + i
        lift_into(meta_ref, q, left_ref[q], ordered_ref, x_ref, i * 256)
    y_ref[...] = dot(x_ref[...], mix_ref[...]).astype(bf16)
    for i in range(2):
        q = g * 2 + i
        spread = spread_ref[q]
        part = (iota((BS, 4 * WIDE), 1) >> 5) & 3
        for k in range(4):
            rk_ref[k * 64 : k * 64 + 64, :] = jnp.where(part == k, spread, jnp.zeros_like(spread))
        keep = keep_of(meta_ref, q, 256)
        for r_hi in range(2):
            rows = jnp.concatenate(
                [y_ref[i * 256 + k * 64 : i * 256 + k * 64 + 64, r_hi * WIDE : r_hi * WIDE + WIDE] for k in range(4)],
                axis=1,
            )
            applied = dot(rows, rk_ref[...], ((1,), (1,)))
            state = bond_ref[q, :, r_hi * 256 : r_hi * 256 + 256].astype(f32)
            trial = jnp.where(keep, state - relax_step * applied, 0.0)
            total_ref[...] += trial * trial
            state_ref[q + 1, :, r_hi * 256 : r_hi * 256 + 256] = (trial * lift_scale).astype(bf16)


def handed_sector(meta_ref, q, left, state_ref, x_ref):
    lift_into(meta_ref, q, left, state_ref, x_ref)
    own = state_ref[q + 1]
    stacked = jnp.concatenate([own[:, k * 128 : k * 128 + 128] for k in range(4)], axis=0)
    both = dot(stacked, x_ref[:256, :], ((0,), (0,)))
    low = iota((BS, 128), 1) < 64
    out = []
    for w in range(0, W, 2):
        a0, b0 = both[:64, w * 128 : w * 128 + 128], both[64:, w * 128 : w * 128 + 128]
        a1, b1 = both[:64, w * 128 + 128 : w * 128 + 256], both[64:, w * 128 + 128 : w * 128 + 256]
        out.append(jnp.where(low, a0, b1) + pltpu.roll(jnp.where(low, a1, b0), 64, 1))
    return jnp.concatenate(out, axis=1)


def kernel(segs, blks, count, meta_in, bond_in, left_in, right_in, mpo_ref, out_ref,
           meta_land, meta_ref, bond_ref, left_ref, right_ref, spread_ref, ordered_ref, state_ref,
           halo_ref, lane_ref, order_ref, mix_ref, x_ref, y_ref, rk_ref, total_ref, sums_ref, raw_ref,
           local_sem, bond_send, bond_recv, left_send, left_recv, meta_sem, halo_send, halo_recv, sum_send, sum_recv):
    seg, blk = lax.axis_index("seg"), lax.axis_index("blk")
    ahead, behind = lax.rem(seg + 1, segs), lax.rem(seg + segs - 1, segs)
    up, down = lax.rem(blk + 1, blks), lax.rem(blk + blks - 1, blks)
    sectors = bond_ref.shape[0]
    groups = sectors // 2

    def remote(src, dst, send, recv, where):
        return pltpu.make_async_remote_copy(
            src_ref=src, dst_ref=dst, send_sem=send, recv_sem=recv, device_id=where,
            device_id_type=pl.DeviceIdType.MESH,
        )

    def bond_copy(g):
        part = pl.ds(g * 2, 2)
        return remote(bond_in.at[part], bond_ref.at[part], bond_send.at[g], bond_recv.at[g], {"seg": ahead})

    def left_copy(g):
        part = pl.ds(g * 2, 2)
        return remote(left_in.at[part], left_ref.at[part], left_send.at[g], left_recv.at[g], {"seg": ahead})

    def halo_copy(i, src):
        return remote(src, halo_ref.at[i], halo_send.at[i], halo_recv.at[i], {"blk": up if i % 2 == 0 else down})

    def sum_copy(k):
        return remote(sums_ref.at[0], sums_ref.at[k], sum_send.at[k], sum_recv.at[k], {"blk": lax.rem(blk + k, blks)})

    barrier = pltpu.get_barrier_semaphore()
    for where in [{"seg": ahead}, {"seg": behind}] + [{"blk": lax.rem(blk + k, blks)} for k in range(1, blks)]:
        pl.semaphore_signal(barrier, inc=1, device_id=where, device_id_type=pl.DeviceIdType.MESH)
    pl.semaphore_wait(barrier, blks + 1)

    meta_copy = remote(meta_in, meta_land, meta_sem.at[0], meta_sem.at[1], {"seg": ahead})
    meta_copy.start()
    bond_copy(groups - 1).start()
    bond_copy(0).start()
    bond_copy(1).start()
    left_copy(0).start()
    bond_copy(2).start()
    left_copy(1).start()
    right_copy = pltpu.make_async_copy(right_in, right_ref, local_sem.at[0])
    right_copy.start()
    order_state(lane_ref)
    total_ref[...] = jnp.zeros_like(total_ref)
    meta_copy.wait_recv()
    to_smem = pltpu.make_async_copy(meta_land, meta_ref, local_sem.at[1])
    to_smem.start()
    to_smem.wait()

    def prepare(g):
        for i in range(2):
            q = g * 2 + i
            held = jnp.where(keep_of(meta_ref, q, LANES), bond_ref[q].astype(f32), 0.0).astype(bf16)
            ordered_ref[q + 1] = dot(held, lane_ref[...]).astype(bf16)

    bond_copy(groups - 1).wait_recv()
    prepare(groups - 1)
    first = halo_copy(0, ordered_ref.at[sectors])
    first.start()
    bond_copy(0).wait_recv()
    prepare(0)
    last = halo_copy(1, ordered_ref.at[1])
    last.start()
    spread_operator(mpo_ref, mix_ref)
    order_right(order_ref)
    right_copy.wait()

    def spread_right(q, carry):
        spread_ref[q] = dot(right_ref[q], order_ref[...]).astype(bf16)
        return carry

    lax.fori_loop(0, sectors, spread_right, 0)
    first.wait_recv()
    last.wait_recv()
    low_edge = (blk > 0).astype(f32)
    high_edge = (blk < blks - 1).astype(f32)
    ordered_ref[0] = (halo_ref[0].astype(f32) * low_edge).astype(bf16)
    ordered_ref[sectors + 1] = (halo_ref[1].astype(f32) * high_edge).astype(bf16)

    def handed_pair(g):
        for i in range(2):
            q = g * 2 + i
            raw_ref[q] = handed_sector(meta_ref, q, left_ref[q], state_ref, x_ref)

    def step(g, carry):
        @pl.when(g + 3 < groups - 1)
        def _():
            bond_copy(g + 3).start()

        @pl.when(g + 2 < groups)
        def _():
            left_copy(g + 2).start()

        @pl.when(g + 1 < groups - 1)
        def _():
            bond_copy(g + 1).wait_recv()
            prepare(g + 1)

        left_copy(g).wait_recv()
        relax_pair(meta_ref, g, left_ref, spread_ref, bond_ref, ordered_ref, mix_ref, x_ref, y_ref, rk_ref,
                   state_ref, total_ref)

        @pl.when(g == 0)
        def _():
            halo_copy(3, state_ref.at[1]).start()

        @pl.when(g == groups - 1)
        def _():
            halo_copy(2, state_ref.at[sectors]).start()
            total = total_ref[...]
            part = total[:, :128] + total[:, 128:]
            sums_ref[0] = sum(part[k * 8 : k * 8 + 8] for k in range(8))
            for k in range(1, blks):
                sum_copy(k).start()

        @pl.when(g >= 2)
        def _():
            handed_pair(g - 1)

        return carry

    lax.fori_loop(0, groups, step, 0)
    third, fourth = halo_copy(2, state_ref.at[sectors]), halo_copy(3, state_ref.at[1])
    third.wait_recv()
    fourth.wait_recv()
    state_ref[0] = (halo_ref[2].astype(f32) * low_edge).astype(bf16)
    state_ref[sectors + 1] = (halo_ref[3].astype(f32) * high_edge).astype(bf16)
    lax.fori_loop(0, 2, lambda i, carry: (handed_pair((groups - 1) * (1 - i)), carry)[1], 0)
    for k in range(1, blks):
        sum_copy(k).wait_recv()
    total = sums_ref[0]
    for k in range(1, blks):
        total += sums_ref[k]
    mean_square = jnp.sum(jnp.sum(total, axis=1, keepdims=True), axis=0, keepdims=True) / count
    scale = 1.0 / ((mean_square + epsilon) * (lift_scale * lift_scale * math.sqrt(BS * P_SIZE)))

    def finish(q, carry):
        out_ref[q] = (raw_ref[q] * scale).astype(bf16)
        return carry

    lax.fori_loop(0, sectors, finish, 0)
    meta_copy.wait_send()
    for copy in (first, last, third, fourth):
        copy.wait_send()
    for k in range(1, blks):
        sum_copy(k).wait_send()

    def drain(g, carry):
        bond_copy(g).wait_send()
        left_copy(g).wait_send()
        return carry

    lax.fori_loop(0, groups, drain, 0)


def shards(bond_tensor, left_env, right_env, kept_dims, sector_links, mpo_pair):
    segs, blks = lax.axis_size("seg"), lax.axis_size("blk")
    sectors = left_env.shape[1]
    meta = jnp.concatenate([sector_links[0], kept_dims[0].T], axis=1)
    meta = jnp.pad(meta, ((0, 0), (0, 128 - W - 2)))
    count = sectors * blks * BS * P_SIZE * BS
    anywhere = pl.BlockSpec(memory_space=pl.ANY)
    vmem = pl.BlockSpec(memory_space=pltpu.VMEM)
    dma = pltpu.SemaphoreType.DMA
    out = pl.pallas_call(
        functools.partial(kernel, segs, blks, count),
        out_shape=jax.ShapeDtypeStruct((sectors, BS, WIDE), bf16),
        in_specs=[anywhere, anywhere, anywhere, anywhere, vmem],
        out_specs=vmem,
        scratch_shapes=[
            pltpu.VMEM((sectors, 128), jnp.int32),
            pltpu.SMEM((sectors, 128), jnp.int32),
            pltpu.VMEM((sectors, BS, LANES), bf16),
            pltpu.VMEM((sectors, BS, WIDE), bf16),
            pltpu.VMEM((sectors, BS, WIDE), bf16),
            pltpu.VMEM((sectors, BS, 4 * WIDE), bf16),
            pltpu.VMEM((sectors + 2, BS, LANES), bf16),
            pltpu.VMEM((sectors + 2, BS, LANES), bf16),
            pltpu.VMEM((4, BS, LANES), bf16),
            pltpu.VMEM((LANES, LANES), bf16),
            pltpu.VMEM((WIDE, 4 * WIDE), bf16),
            pltpu.VMEM((MIX, MIX), bf16),
            pltpu.VMEM((512, MIX), bf16),
            pltpu.VMEM((512, MIX), bf16),
            pltpu.VMEM((256, 4 * WIDE), bf16),
            pltpu.VMEM((BS, 256), f32),
            pltpu.VMEM((blks, 8, 128), f32),
            pltpu.VMEM((sectors, BS, WIDE), f32),
            dma((2,)),
            dma((sectors // 2,)),
            dma((sectors // 2,)),
            dma((sectors // 2,)),
            dma((sectors // 2,)),
            dma((2,)),
            dma((4,)),
            dma((4,)),
            dma((blks,)),
            dma((blks,)),
        ],
        compiler_params=pltpu.CompilerParams(
            collective_id=0, has_side_effects=True, vmem_limit_bytes=56 * 2**20
        ),
    )(meta, bond_tensor[0], left_env[0], right_env[0], mpo_pair)
    return out[None]


def solution(mesh):
    return jax.shard_map(
        shards,
        mesh=mesh,
        in_specs=(
            P(("runs", "seg"), "blk", None, None),
            P(("runs", "seg"), "blk", None, None),
            P(("runs", "seg"), "blk", None, None),
            P(("runs", "seg"), None, "blk"),
            P(("runs", "seg"), "blk", None),
            P(),
        ),
        out_specs=P(("runs", "seg"), "blk", None, None),
        check_vma=False,
    )
```

```python
import functools
import math

import jax
import jax.numpy as jnp
from jax import lax
from jax.experimental import pallas as pl
from jax.experimental.pallas import tpu as pltpu
from jax.sharding import PartitionSpec as P

BS = 64
P_SIZE = 8
W = 10
LANES = P_SIZE * BS
WIDE = W * BS
MIX = W * 128

relax_step = 0.5
epsilon = 1e-06
lift_scale = 1024.0

f32 = jnp.float32
bf16 = jnp.bfloat16


def iota(shape, dim):
    return lax.broadcasted_iota(jnp.int32, shape, dim)


def dot(a, b, dims=((1,), (0,))):
    return lax.dot_general(a, b, (dims, ((), ())), preferred_element_type=f32)


def order_state(order_ref):
    row, lane = iota((LANES, LANES), 0), iota((LANES, LANES), 1)
    source = ((lane >> 4) & 7) * 64 + (lane >> 7) * 16 + (lane & 15)
    order_ref[...] = (row == source).astype(f32).astype(bf16)


def order_right(order_ref):
    row, lane = iota((WIDE, 128), 0), iota((WIDE, 128), 1)
    for b_hi in range(4):
        for v_hi in range(5):
            source = (v_hi * 2 + ((lane >> 4) & 1)) * 64 + b_hi * 16 + (lane & 15)
            at = (b_hi * 5 + v_hi) * 128
            order_ref[:, at : at + 128] = (row == source).astype(f32).astype(bf16)


def spread_operator(mpo_ref, mix_ref):
    size = W * P_SIZE
    rows = (iota((MIX, size), 1) == (iota((MIX, size), 0) >> 4)).astype(f32).astype(bf16)
    tall = dot(rows, mpo_ref[...]).astype(bf16)
    same = (iota((MIX, 128), 0) & 15) == (iota((MIX, 128), 1) & 15)
    row, lane = iota((size, 128), 0), iota((size, 128), 1)
    for r_hi in range(2):
        for v_hi in range(5):
            column = (v_hi * 2 + ((lane >> 4) & 1)) * 8 + r_hi * 4 + ((lane >> 5) & 3)
            pick = (row == column).astype(f32).astype(bf16)
            at = (r_hi * 5 + v_hi) * 128
            mix_ref[:, at : at + 128] = jnp.where(same, dot(tall, pick), 0.0).astype(bf16)


def keep_of(meta_ref, q, lanes):
    rows = iota((BS, lanes), 0) < meta_ref[q, W]
    columns = (iota((BS, lanes), 1) & 63) < meta_ref[q, W + 1]
    return rows & columns


def place_left(meta_ref, q, left_ref, block_ref):
    half = iota((BS, 256), 1) >> 6
    for w in range(W):
        piece = left_ref[q, :, w * 64 : w * 64 + 64]
        wide = jnp.concatenate([piece] * 4, axis=1)
        block_ref[q, w * 64 : w * 64 + 64, :] = jnp.where(half == meta_ref[q, w] + 1, wide, jnp.zeros_like(wide))


def lift_into(q, block_ref, state_ref, target_ref, base=0):
    source = state_ref[pl.ds(q, 3)].reshape(3 * BS, LANES)
    out = dot(block_ref[q, :, :192], source).astype(bf16)
    for w in range(W):
        for k in range(4):
            target_ref[base + k * 64 : base + k * 64 + 64, w * 128 : w * 128 + 128] = (
                out[w * 64 : w * 64 + 64, k * 128 : k * 128 + 128]
            )


def relax_pair(meta_ref, g, left_ref, block_ref, spread_ref, bond_ref, ordered_ref, mix_ref, x_ref, y_ref, rk_ref, state_ref, total_ref):
    for i in range(2):
        q = g * 2 + i
        place_left(meta_ref, q, left_ref, block_ref)
        lift_into(q, block_ref, ordered_ref, x_ref, i * 256)
    y_ref[...] = dot(x_ref[...], mix_ref[...]).astype(bf16)
    for i in range(2):
        q = g * 2 + i
        spread = spread_ref[q]
        part = (iota((BS, 4 * WIDE), 1) >> 5) & 3
        for k in range(4):
            rk_ref[k * 64 : k * 64 + 64, :] = jnp.where(part == k, spread, jnp.zeros_like(spread))
        keep = keep_of(meta_ref, q, 256)
        rows = [
            jnp.concatenate(
                [y_ref[i * 256 + k * 64 : i * 256 + k * 64 + 64, r_hi * WIDE : r_hi * WIDE + WIDE] for k in range(4)],
                axis=1,
            )
            for r_hi in range(2)
        ]
        both = dot(jnp.concatenate(rows, axis=0), rk_ref[...], ((1,), (1,)))
        for r_hi in range(2):
            applied = both[r_hi * 64 : r_hi * 64 + 64]
            state = bond_ref[q, :, r_hi * 256 : r_hi * 256 + 256].astype(f32)
            trial = jnp.where(keep, state - relax_step * applied, 0.0)
            total_ref[...] += trial * trial
            state_ref[q + 1, :, r_hi * 256 : r_hi * 256 + 256] = (trial * lift_scale).astype(bf16)


def handed_sector(q, block_ref, state_ref, x_ref):
    lift_into(q, block_ref, state_ref, x_ref)
    own = state_ref[q + 1]
    stacked = jnp.concatenate([own[:, k * 128 : k * 128 + 128] for k in range(4)], axis=0)
    both = dot(stacked, x_ref[:256, :], ((0,), (0,)))
    low = iota((BS, 128), 1) < 64
    out = []
    for w in range(0, W, 2):
        a0, b0 = both[:64, w * 128 : w * 128 + 128], both[64:, w * 128 : w * 128 + 128]
        a1, b1 = both[:64, w * 128 + 128 : w * 128 + 256], both[64:, w * 128 + 128 : w * 128 + 256]
        out.append(jnp.where(low, a0, b1) + pltpu.roll(jnp.where(low, a1, b0), 64, 1))
    return jnp.concatenate(out, axis=1)


def kernel(segs, blks, count, meta_in, bond_in, left_in, right_in, mpo_ref, raw_ref, scale_ref,
           meta_land, meta_ref, bond_ref, left_ref, right_ref, spread_ref, ordered_ref, state_ref,
           halo_ref, lane_ref, order_ref, mix_ref, x_ref, y_ref, rk_ref, total_ref, sums_ref, block_ref,
           local_sem, bond_send, bond_recv, left_send, left_recv, meta_sem, halo_send, halo_recv, sum_send, sum_recv):
    seg, blk = lax.axis_index("seg"), lax.axis_index("blk")
    ahead, behind = lax.rem(seg + 1, segs), lax.rem(seg + segs - 1, segs)
    up, down = lax.rem(blk + 1, blks), lax.rem(blk + blks - 1, blks)
    sectors = bond_ref.shape[0]
    groups = sectors // 2

    def remote(src, dst, send, recv, where):
        return pltpu.make_async_remote_copy(
            src_ref=src, dst_ref=dst, send_sem=send, recv_sem=recv, device_id=where,
            device_id_type=pl.DeviceIdType.MESH,
        )

    def bond_copy(g):
        part = pl.ds(g * 2, 2)
        return remote(bond_in.at[part], bond_ref.at[part], bond_send.at[g], bond_recv.at[g], {"seg": ahead})

    def left_copy(g):
        part = pl.ds(g * 2, 2)
        return remote(left_in.at[part], left_ref.at[part], left_send.at[g], left_recv.at[g], {"seg": ahead})

    def halo_copy(i, src):
        return remote(src, halo_ref.at[i], halo_send.at[i], halo_recv.at[i], {"blk": up if i % 2 == 0 else down})

    def sum_copy(k):
        return remote(sums_ref.at[0], sums_ref.at[k], sum_send.at[k], sum_recv.at[k], {"blk": lax.rem(blk + k, blks)})

    barrier = pltpu.get_barrier_semaphore()
    for where in [{"seg": ahead}, {"seg": behind}] + [{"blk": lax.rem(blk + k, blks)} for k in range(1, blks)]:
        pl.semaphore_signal(barrier, inc=1, device_id=where, device_id_type=pl.DeviceIdType.MESH)
    pl.semaphore_wait(barrier, blks + 1)

    meta_copy = remote(meta_in, meta_land, meta_sem.at[0], meta_sem.at[1], {"seg": ahead})
    meta_copy.start()
    bond_copy(groups - 1).start()
    bond_copy(0).start()
    bond_copy(1).start()
    left_copy(0).start()
    bond_copy(2).start()
    left_copy(1).start()
    right_copy = pltpu.make_async_copy(right_in, right_ref, local_sem.at[0])
    right_copy.start()
    order_state(lane_ref)
    total_ref[...] = jnp.zeros_like(total_ref)
    meta_copy.wait_recv()
    to_smem = pltpu.make_async_copy(meta_land, meta_ref, local_sem.at[1])
    to_smem.start()
    to_smem.wait()

    def prepare(g):
        for i in range(2):
            q = g * 2 + i
            held = jnp.where(keep_of(meta_ref, q, LANES), bond_ref[q].astype(f32), 0.0).astype(bf16)
            ordered_ref[q + 1] = dot(held, lane_ref[...]).astype(bf16)

    bond_copy(groups - 1).wait_recv()
    prepare(groups - 1)
    first = halo_copy(0, ordered_ref.at[sectors])
    first.start()
    bond_copy(0).wait_recv()
    prepare(0)
    last = halo_copy(1, ordered_ref.at[1])
    last.start()
    spread_operator(mpo_ref, mix_ref)
    order_right(order_ref)
    right_copy.wait()

    def spread_right(q, carry):
        spread_ref[q] = dot(right_ref[q], order_ref[...]).astype(bf16)
        return carry

    lax.fori_loop(0, sectors, spread_right, 0)
    first.wait_recv()
    last.wait_recv()
    low_edge = (blk > 0).astype(f32)
    high_edge = (blk < blks - 1).astype(f32)
    ordered_ref[0] = (halo_ref[0].astype(f32) * low_edge).astype(bf16)
    ordered_ref[sectors + 1] = (halo_ref[1].astype(f32) * high_edge).astype(bf16)

    def hand(q):
        raw_ref[q] = handed_sector(q, block_ref, state_ref, x_ref)

    def step(g, carry):
        @pl.when(g + 3 < groups - 1)
        def _():
            bond_copy(g + 3).start()

        @pl.when(g + 2 < groups)
        def _():
            left_copy(g + 2).start()

        @pl.when(g + 1 < groups - 1)
        def _():
            bond_copy(g + 1).wait_recv()
            prepare(g + 1)

        left_copy(g).wait_recv()
        relax_pair(meta_ref, g, left_ref, block_ref, spread_ref, bond_ref, ordered_ref, mix_ref, x_ref, y_ref, rk_ref,
                   state_ref, total_ref)

        @pl.when(g == 0)
        def _():
            halo_copy(3, state_ref.at[1]).start()

        @pl.when(g == groups - 1)
        def _():
            halo_copy(2, state_ref.at[sectors]).start()
            total = total_ref[...]
            part = total[:, :128] + total[:, 128:]
            sums_ref[0] = sum(part[k * 8 : k * 8 + 8] for k in range(8))
            for k in range(1, blks):
                sum_copy(k).start()

        @pl.when(g >= 1)
        def _():
            hand(g * 2 - 1)
            hand(g * 2)

        return carry

    lax.fori_loop(0, groups, step, 0)
    third, fourth = halo_copy(2, state_ref.at[sectors]), halo_copy(3, state_ref.at[1])
    third.wait_recv()
    fourth.wait_recv()
    state_ref[0] = (halo_ref[2].astype(f32) * low_edge).astype(bf16)
    state_ref[sectors + 1] = (halo_ref[3].astype(f32) * high_edge).astype(bf16)
    hand(sectors - 1)
    hand(0)
    for k in range(1, blks):
        sum_copy(k).wait_recv()
    total = sums_ref[0]
    for k in range(1, blks):
        total += sums_ref[k]
    mean_square = jnp.sum(jnp.sum(total, axis=1, keepdims=True), axis=0, keepdims=True) / count
    scale = 1.0 / ((mean_square + epsilon) * (lift_scale * lift_scale * math.sqrt(BS * P_SIZE)))

    scale_ref[...] = jnp.broadcast_to(scale, scale_ref.shape)
    meta_copy.wait_send()
    for copy in (first, last, third, fourth):
        copy.wait_send()
    for k in range(1, blks):
        sum_copy(k).wait_send()

    def drain(g, carry):
        bond_copy(g).wait_send()
        left_copy(g).wait_send()
        return carry

    lax.fori_loop(0, groups, drain, 0)


def shards(bond_tensor, left_env, right_env, kept_dims, sector_links, mpo_pair):
    segs, blks = lax.axis_size("seg"), lax.axis_size("blk")
    sectors = left_env.shape[1]
    meta = jnp.concatenate([sector_links[0], kept_dims[0].T], axis=1)
    meta = jnp.pad(meta, ((0, 0), (0, 128 - W - 2)))
    count = sectors * blks * BS * P_SIZE * BS
    anywhere = pl.BlockSpec(memory_space=pl.ANY)
    vmem = pl.BlockSpec(memory_space=pltpu.VMEM)
    dma = pltpu.SemaphoreType.DMA
    raw, scale = pl.pallas_call(
        functools.partial(kernel, segs, blks, count),
        out_shape=(jax.ShapeDtypeStruct((sectors, BS, WIDE), f32), jax.ShapeDtypeStruct((8, 128), f32)),
        in_specs=[anywhere, anywhere, anywhere, anywhere, vmem],
        out_specs=(vmem, vmem),
        scratch_shapes=[
            pltpu.VMEM((sectors, 128), jnp.int32),
            pltpu.SMEM((sectors, 128), jnp.int32),
            pltpu.VMEM((sectors, BS, LANES), bf16),
            pltpu.VMEM((sectors, BS, WIDE), bf16),
            pltpu.VMEM((sectors, BS, WIDE), bf16),
            pltpu.VMEM((sectors, BS, 4 * WIDE), bf16),
            pltpu.VMEM((sectors + 2, BS, LANES), bf16),
            pltpu.VMEM((sectors + 2, BS, LANES), bf16),
            pltpu.VMEM((4, BS, LANES), bf16),
            pltpu.VMEM((LANES, LANES), bf16),
            pltpu.VMEM((WIDE, 4 * WIDE), bf16),
            pltpu.VMEM((MIX, MIX), bf16),
            pltpu.VMEM((512, MIX), bf16),
            pltpu.VMEM((512, MIX), bf16),
            pltpu.VMEM((256, 4 * WIDE), bf16),
            pltpu.VMEM((BS, 256), f32),
            pltpu.VMEM((blks, 8, 128), f32),
            pltpu.VMEM((sectors, WIDE, 256), bf16),
            dma((2,)),
            dma((sectors // 2,)),
            dma((sectors // 2,)),
            dma((sectors // 2,)),
            dma((sectors // 2,)),
            dma((2,)),
            dma((4,)),
            dma((4,)),
            dma((blks,)),
            dma((blks,)),
        ],
        compiler_params=pltpu.CompilerParams(
            collective_id=0, has_side_effects=True, vmem_limit_bytes=56 * 2**20
        ),
    )(meta, bond_tensor[0], left_env[0], right_env[0], mpo_pair)
    return (raw * scale[0, 0]).astype(bf16)[None]


def solution(mesh):
    return jax.shard_map(
        shards,
        mesh=mesh,
        in_specs=(
            P(("runs", "seg"), "blk", None, None),
            P(("runs", "seg"), "blk", None, None),
            P(("runs", "seg"), "blk", None, None),
            P(("runs", "seg"), None, "blk"),
            P(("runs", "seg"), "blk", None),
            P(),
        ),
        out_specs=P(("runs", "seg"), "blk", None, None),
        check_vma=False,
    )
```

```python
import functools
import math

import jax
import jax.numpy as jnp
from jax import lax
from jax.experimental import pallas as pl
from jax.experimental.pallas import tpu as pltpu
from jax.sharding import PartitionSpec as P

BS = 64
P_SIZE = 8
W = 10
LANES = P_SIZE * BS
WIDE = W * BS
MIX = W * 128

relax_step = 0.5
epsilon = 1e-06
lift_scale = 1024.0

f32 = jnp.float32
bf16 = jnp.bfloat16


def iota(shape, dim):
    return lax.broadcasted_iota(jnp.int32, shape, dim)


def dot(a, b, dims=((1,), (0,))):
    return lax.dot_general(a, b, (dims, ((), ())), preferred_element_type=f32)


def order_state(order_ref):
    row, lane = iota((LANES, LANES), 0), iota((LANES, LANES), 1)
    source = ((lane >> 4) & 7) * 64 + (lane >> 7) * 16 + (lane & 15)
    order_ref[...] = (row == source).astype(f32).astype(bf16)


def order_right(order_ref):
    row, lane = iota((WIDE, 128), 0), iota((WIDE, 128), 1)
    for b_hi in range(4):
        for v_hi in range(5):
            source = (v_hi * 2 + ((lane >> 4) & 1)) * 64 + b_hi * 16 + (lane & 15)
            at = (b_hi * 5 + v_hi) * 128
            order_ref[:, at : at + 128] = (row == source).astype(f32).astype(bf16)


def spread_operator(mpo_ref, mix_ref):
    size = W * P_SIZE
    rows = (iota((MIX, size), 1) == (iota((MIX, size), 0) >> 4)).astype(f32).astype(bf16)
    tall = dot(rows, mpo_ref[...]).astype(bf16)
    same = (iota((MIX, 128), 0) & 15) == (iota((MIX, 128), 1) & 15)
    row, lane = iota((size, 128), 0), iota((size, 128), 1)
    for r_hi in range(2):
        for v_hi in range(5):
            column = (v_hi * 2 + ((lane >> 4) & 1)) * 8 + r_hi * 4 + ((lane >> 5) & 3)
            pick = (row == column).astype(f32).astype(bf16)
            at = (r_hi * 5 + v_hi) * 128
            mix_ref[:, at : at + 128] = jnp.where(same, dot(tall, pick), 0.0).astype(bf16)


def keep_of(meta_ref, q, lanes):
    rows = iota((BS, lanes), 0) < meta_ref[q, W]
    columns = (iota((BS, lanes), 1) & 63) < meta_ref[q, W + 1]
    return rows & columns


def place_left(meta_ref, q, left_ref, block_ref):
    half = iota((BS, 256), 1) >> 6
    for w in range(W):
        piece = left_ref[q, :, w * 64 : w * 64 + 64]
        wide = jnp.concatenate([piece] * 4, axis=1)
        block_ref[q, w * 64 : w * 64 + 64, :] = jnp.where(half == meta_ref[q, w] + 1, wide, jnp.zeros_like(wide))


def lift_into(q, block_ref, state_ref, target_ref, base=0):
    source = state_ref[pl.ds(q, 3)].reshape(3 * BS, LANES)
    out = dot(block_ref[q, :, :192], source).astype(bf16)
    for w in range(W):
        for k in range(4):
            target_ref[base + k * 64 : base + k * 64 + 64, w * 128 : w * 128 + 128] = (
                out[w * 64 : w * 64 + 64, k * 128 : k * 128 + 128]
            )


def relax_pair(meta_ref, g, left_ref, block_ref, spread_ref, bond_ref, ordered_ref, mix_ref, x_ref, y_ref, rk_ref, state_ref, total_ref):
    for i in range(2):
        q = g * 2 + i
        place_left(meta_ref, q, left_ref, block_ref)
        lift_into(q, block_ref, ordered_ref, x_ref, i * 256)
    y_ref[...] = dot(x_ref[...], mix_ref[...]).astype(bf16)
    for i in range(2):
        q = g * 2 + i
        spread = spread_ref[q]
        part = (iota((BS, 4 * WIDE), 1) >> 5) & 3
        for k in range(4):
            rk_ref[k * 64 : k * 64 + 64, :] = jnp.where(part == k, spread, jnp.zeros_like(spread))
        keep = keep_of(meta_ref, q, 256)
        rows = [
            jnp.concatenate(
                [y_ref[i * 256 + k * 64 : i * 256 + k * 64 + 64, r_hi * WIDE : r_hi * WIDE + WIDE] for k in range(4)],
                axis=1,
            )
            for r_hi in range(2)
        ]
        both = dot(jnp.concatenate(rows, axis=0), rk_ref[...], ((1,), (1,)))
        for r_hi in range(2):
            applied = both[r_hi * 64 : r_hi * 64 + 64]
            state = bond_ref[q, :, r_hi * 256 : r_hi * 256 + 256].astype(f32)
            trial = jnp.where(keep, state - relax_step * applied, 0.0)
            total_ref[...] += trial * trial
            state_ref[q + 1, :, r_hi * 256 : r_hi * 256 + 256] = (trial * lift_scale).astype(bf16)


def handed_sector(q, block_ref, state_ref, x_ref):
    lift_into(q, block_ref, state_ref, x_ref)
    own = state_ref[q + 1]
    stacked = jnp.concatenate([own[:, k * 128 : k * 128 + 128] for k in range(4)], axis=0)
    both = dot(stacked, x_ref[:256, :], ((0,), (0,)))
    low = iota((BS, 128), 1) < 64
    out = []
    for w in range(0, W, 2):
        a0, b0 = both[:64, w * 128 : w * 128 + 128], both[64:, w * 128 : w * 128 + 128]
        a1, b1 = both[:64, w * 128 + 128 : w * 128 + 256], both[64:, w * 128 + 128 : w * 128 + 256]
        out.append(jnp.where(low, a0, b1) + pltpu.roll(jnp.where(low, a1, b0), 64, 1))
    return jnp.concatenate(out, axis=1)


def kernel(segs, blks, count, meta_in, bond_in, left_in, right_in, mpo_ref, out_ref,
           meta_land, meta_ref, bond_ref, left_ref, right_ref, spread_ref, ordered_ref, state_ref,
           halo_ref, lane_ref, order_ref, mix_ref, x_ref, y_ref, rk_ref, total_ref, sums_ref, block_ref, raw_ref,
           local_sem, bond_send, bond_recv, left_send, left_recv, meta_sem, halo_send, halo_recv, sum_send, sum_recv):
    seg, blk = lax.axis_index("seg"), lax.axis_index("blk")
    ahead, behind = lax.rem(seg + 1, segs), lax.rem(seg + segs - 1, segs)
    up, down = lax.rem(blk + 1, blks), lax.rem(blk + blks - 1, blks)
    sectors = bond_ref.shape[0]
    groups = sectors // 2

    def remote(src, dst, send, recv, where):
        return pltpu.make_async_remote_copy(
            src_ref=src, dst_ref=dst, send_sem=send, recv_sem=recv, device_id=where,
            device_id_type=pl.DeviceIdType.MESH,
        )

    def bond_copy(g):
        part = pl.ds(g * 2, 2)
        return remote(bond_in.at[part], bond_ref.at[part], bond_send.at[g], bond_recv.at[g], {"seg": ahead})

    def left_copy(g):
        part = pl.ds(g * 2, 2)
        return remote(left_in.at[part], left_ref.at[part], left_send.at[g], left_recv.at[g], {"seg": ahead})

    def halo_copy(i, src):
        return remote(src, halo_ref.at[i], halo_send.at[i], halo_recv.at[i], {"blk": up if i % 2 == 0 else down})

    def sum_copy(k):
        return remote(sums_ref.at[0], sums_ref.at[k], sum_send.at[k], sum_recv.at[k], {"blk": lax.rem(blk + k, blks)})

    barrier = pltpu.get_barrier_semaphore()
    for where in [{"seg": ahead}, {"seg": behind}] + [{"blk": lax.rem(blk + k, blks)} for k in range(1, blks)]:
        pl.semaphore_signal(barrier, inc=1, device_id=where, device_id_type=pl.DeviceIdType.MESH)
    pl.semaphore_wait(barrier, blks + 1)

    meta_copy = remote(meta_in, meta_land, meta_sem.at[0], meta_sem.at[1], {"seg": ahead})
    meta_copy.start()
    bond_copy(groups - 1).start()
    bond_copy(0).start()
    bond_copy(1).start()
    left_copy(0).start()
    bond_copy(2).start()
    left_copy(1).start()
    right_copy = pltpu.make_async_copy(right_in, right_ref, local_sem.at[0])
    right_copy.start()
    order_state(lane_ref)
    total_ref[...] = jnp.zeros_like(total_ref)
    spread_operator(mpo_ref, mix_ref)
    order_right(order_ref)
    right_copy.wait()

    def spread_right(q, carry):
        spread_ref[q] = dot(right_ref[q], order_ref[...]).astype(bf16)
        return carry

    lax.fori_loop(0, sectors, spread_right, 0)
    meta_copy.wait_recv()
    to_smem = pltpu.make_async_copy(meta_land, meta_ref, local_sem.at[1])
    to_smem.start()
    to_smem.wait()

    def prepare(g):
        for i in range(2):
            q = g * 2 + i
            held = jnp.where(keep_of(meta_ref, q, LANES), bond_ref[q].astype(f32), 0.0).astype(bf16)
            ordered_ref[q + 1] = dot(held, lane_ref[...]).astype(bf16)

    bond_copy(groups - 1).wait_recv()
    prepare(groups - 1)
    first = halo_copy(0, ordered_ref.at[sectors])
    first.start()
    bond_copy(0).wait_recv()
    prepare(0)
    last = halo_copy(1, ordered_ref.at[1])
    last.start()
    first.wait_recv()
    last.wait_recv()
    low_edge = (blk > 0).astype(f32)
    high_edge = (blk < blks - 1).astype(f32)
    ordered_ref[0] = (halo_ref[0].astype(f32) * low_edge).astype(bf16)
    ordered_ref[sectors + 1] = (halo_ref[1].astype(f32) * high_edge).astype(bf16)

    def hand(q):
        raw_ref[q] = handed_sector(q, block_ref, state_ref, x_ref)

    def step(g, carry):
        @pl.when(g + 3 < groups - 1)
        def _():
            bond_copy(g + 3).start()

        @pl.when(g + 2 < groups)
        def _():
            left_copy(g + 2).start()

        @pl.when(g + 1 < groups - 1)
        def _():
            bond_copy(g + 1).wait_recv()
            prepare(g + 1)

        left_copy(g).wait_recv()
        relax_pair(meta_ref, g, left_ref, block_ref, spread_ref, bond_ref, ordered_ref, mix_ref, x_ref, y_ref, rk_ref,
                   state_ref, total_ref)

        @pl.when(g == 0)
        def _():
            halo_copy(3, state_ref.at[1]).start()

        @pl.when(g == groups - 1)
        def _():
            halo_copy(2, state_ref.at[sectors]).start()
            total = total_ref[...]
            part = total[:, :128] + total[:, 128:]
            sums_ref[0] = sum(part[k * 8 : k * 8 + 8] for k in range(8))
            for k in range(1, blks):
                sum_copy(k).start()

        @pl.when(g >= 1)
        def _():
            hand(g * 2 - 1)
            hand(g * 2)

        return carry

    lax.fori_loop(0, groups, step, 0)
    third, fourth = halo_copy(2, state_ref.at[sectors]), halo_copy(3, state_ref.at[1])
    third.wait_recv()
    fourth.wait_recv()
    state_ref[0] = (halo_ref[2].astype(f32) * low_edge).astype(bf16)
    state_ref[sectors + 1] = (halo_ref[3].astype(f32) * high_edge).astype(bf16)
    hand(sectors - 1)
    hand(0)
    for k in range(1, blks):
        sum_copy(k).wait_recv()
    total = sums_ref[0]
    for k in range(1, blks):
        total += sums_ref[k]
    mean_square = jnp.sum(jnp.sum(total, axis=1, keepdims=True), axis=0, keepdims=True) / count
    scale = 1.0 / ((mean_square + epsilon) * (lift_scale * lift_scale * math.sqrt(BS * P_SIZE)))


    def finish(q, carry):
        out_ref[q] = (raw_ref[q] * scale).astype(bf16)
        return carry

    lax.fori_loop(0, sectors, finish, 0)
    meta_copy.wait_send()
    for copy in (first, last, third, fourth):
        copy.wait_send()
    for k in range(1, blks):
        sum_copy(k).wait_send()

    def drain(g, carry):
        bond_copy(g).wait_send()
        left_copy(g).wait_send()
        return carry

    lax.fori_loop(0, groups, drain, 0)


def shards(bond_tensor, left_env, right_env, kept_dims, sector_links, mpo_pair):
    segs, blks = lax.axis_size("seg"), lax.axis_size("blk")
    sectors = left_env.shape[1]
    meta = jnp.concatenate([sector_links[0], kept_dims[0].T], axis=1)
    meta = jnp.pad(meta, ((0, 0), (0, 128 - W - 2)))
    count = sectors * blks * BS * P_SIZE * BS
    anywhere = pl.BlockSpec(memory_space=pl.ANY)
    vmem = pl.BlockSpec(memory_space=pltpu.VMEM)
    dma = pltpu.SemaphoreType.DMA
    out = pl.pallas_call(
        functools.partial(kernel, segs, blks, count),
        out_shape=jax.ShapeDtypeStruct((sectors, BS, WIDE), bf16),
        in_specs=[anywhere, anywhere, anywhere, anywhere, vmem],
        out_specs=vmem,
        scratch_shapes=[
            pltpu.VMEM((sectors, 128), jnp.int32),
            pltpu.SMEM((sectors, 128), jnp.int32),
            pltpu.VMEM((sectors, BS, LANES), bf16),
            pltpu.VMEM((sectors, BS, WIDE), bf16),
            pltpu.VMEM((sectors, BS, WIDE), bf16),
            pltpu.VMEM((sectors, BS, 4 * WIDE), bf16),
            pltpu.VMEM((sectors + 2, BS, LANES), bf16),
            pltpu.VMEM((sectors + 2, BS, LANES), bf16),
            pltpu.VMEM((4, BS, LANES), bf16),
            pltpu.VMEM((LANES, LANES), bf16),
            pltpu.VMEM((WIDE, 4 * WIDE), bf16),
            pltpu.VMEM((MIX, MIX), bf16),
            pltpu.VMEM((512, MIX), bf16),
            pltpu.VMEM((512, MIX), bf16),
            pltpu.VMEM((256, 4 * WIDE), bf16),
            pltpu.VMEM((BS, 256), f32),
            pltpu.VMEM((blks, 8, 128), f32),
            pltpu.VMEM((sectors, WIDE, 256), bf16),
            pltpu.VMEM((sectors, BS, WIDE), f32),
            dma((2,)),
            dma((sectors // 2,)),
            dma((sectors // 2,)),
            dma((sectors // 2,)),
            dma((sectors // 2,)),
            dma((2,)),
            dma((4,)),
            dma((4,)),
            dma((blks,)),
            dma((blks,)),
        ],
        compiler_params=pltpu.CompilerParams(
            collective_id=0, has_side_effects=True, vmem_limit_bytes=56 * 2**20
        ),
    )(meta, bond_tensor[0], left_env[0], right_env[0], mpo_pair)
    return out[None]


def solution(mesh):
    return jax.shard_map(
        shards,
        mesh=mesh,
        in_specs=(
            P(("runs", "seg"), "blk", None, None),
            P(("runs", "seg"), "blk", None, None),
            P(("runs", "seg"), "blk", None, None),
            P(("runs", "seg"), None, "blk"),
            P(("runs", "seg"), "blk", None),
            P(),
        ),
        out_specs=P(("runs", "seg"), "blk", None, None),
        check_vma=False,
    )
```
